32 devices in a mesh: lon: 16 (over z, x, core), lat: 2 (over y).
Axes of the slice: x: 2, y: 2, z: 4, core: 2. Of those that a mesh axis runs over, the one named last changes fastest.
Arguments:
- tracer_start: float32 [3, 16, 32, 2048], P(None, None, 'lat', 'lon'), may hold values from -6 to 6
- source: float32 [3, 16, 32, 2048], P(None, None, 'lat', 'lon'), may hold values from -3 to 3
- target: float32 [3, 16, 32, 2048], P(None, None, 'lat', 'lon'), may hold values from -27 to 27
- east_vel: float32 [16, 32, 2048], P(None, 'lat', 'lon'), may hold values from -0.12 to 0.12
- north_vel: float32 [16, 32, 2048], P(None, 'lat', 'lon'), may hold values from -0.12 to 0.12
- vertical_vel: float32 [16, 32, 2048], P(None, 'lat', 'lon'), may hold values from -0.12 to 0.12
- diffusivity: float32 [16, 32, 2048], P(None, 'lat', 'lon'), may hold values from 0.01 to 0.04
- sea_mask: int32 [16, 32, 2048], P(None, 'lat', 'lon'), may hold values 0 or 1
- reaction_rate: float32 [3, 16], replicated, may hold values from 0.05 to 0.5
- fold_partner: int32 [2048], P('lon'), may hold values from 0 to 2047, as said below
Outputs:
- source_grad: float32 [3, 16, 32, 2048], P(None, None, 'lat', 'lon')
- grad_norm: float32 [], replicated
The draws below stay inside these ranges and needn't reach their ends.
Inputs may be any that keep to these rules, and one draw needn't show every extreme that they name: fold_partner[fold_partner[i]] = i; column i meets column (s - i) mod 2048 across the fold, for one s of each draw.
All inputs are finite; a program needn't handle non-finite values. No bound on the sum of `sea_mask` on one device may be relied on, other than what follows from the above.
Results may differ from the reference program's by a relative error of at most 0.00002.
Values sent between devices are 32-bit elements; how exact they have to be, the bound alone decides.
A program may use at most 64 MiB of HBM per device.

```python
import math
import jax
import jax.numpy as jnp
from jax import lax

LEV = 16
NTR = 3
STEPS = 4
NX = 2048
NY = 32


def draw_target(key, part):
    lon_pos = jnp.arange(NX, dtype=jnp.float32) / NX
    lat_pos = jnp.arange(NY, dtype=jnp.float32) / NY
    scale = 0.5 * jnp.exp(jnp.log(3.0) * (lat_pos[:, None] + lon_pos[None, :]))
    base = jnp.clip(jax.random.normal(key, (NTR, LEV, NY, NX), jnp.float32), -6.0, 6.0)
    return base * scale


def draw_fold_partner(key, part):
    offset = jax.random.randint(key, (), 0, NX, dtype=jnp.int32)
    return (offset - jnp.arange(NX, dtype=jnp.int32)) % NX


def plant(array, rng, least, largest):
    longest = array.shape.index(max(array.shape))
    spots = []
    for shift in (0, 1):
        where = [jax.random.randint(jax.random.fold_in(rng, axis), (), 0, length) for axis, length in enumerate(array.shape)]
        where[longest] = (where[longest] + shift) % array.shape[longest]
        spots.append(tuple(where))
    return array.at[spots[0]].set(least).at[spots[1]].set(largest)


def shard_levels(stream_key, dims, shards, least, top_value):
    def one(axis_at, parts):
        steps = jax.random.uniform(jax.random.fold_in(jax.random.fold_in(stream_key, 6), axis_at), (parts,), jnp.float32, least / len(shards), top_value / len(shards))
        return jnp.repeat(jnp.exp(steps), dims[axis_at] // parts).reshape((-1,) + (1,) * (len(dims) - axis_at - 1))

    gain = one(*shards[0])
    for cut in shards[1:]:
        gain = gain * one(*cut)
    return gain


def bell_draw(key, extent, width, reach, pieces=(), kind=jnp.bfloat16):
    loudness = shard_levels(key, extent, pieces, -0.22, 0.18) if pieces else 1.0
    array = jax.random.normal(key, extent, jnp.float32) * width * loudness
    return jnp.minimum(jnp.maximum(array, -reach), reach).astype(kind)


def setup_inputs(seed: int = 0) -> dict:
    key_of = jax.random.split(jax.random.key(seed), 11)
    tracer_start = bell_draw(key_of[0], (NTR, LEV, NY, NX), 1.0, 6.0, ((2, 2), (3, 16)), jnp.float32)
    source = bell_draw(key_of[1], (NTR, LEV, NY, NX), 0.5, 3.0, ((2, 2), (3, 16)), jnp.float32)
    target = draw_target(jax.random.fold_in(key_of[10], 71), 0)
    east_vel = jnp.clip(jax.random.uniform(key_of[3], (LEV, NY, NX), jnp.float32, -0.12, 0.12) * shard_levels(key_of[3], (LEV, NY, NX), ((1, 2), (2, 16)), -0.4, 0.0), -0.12, 0.12)
    north_vel = jnp.clip(jax.random.uniform(key_of[4], (LEV, NY, NX), jnp.float32, -0.12, 0.12) * shard_levels(key_of[4], (LEV, NY, NX), ((1, 2), (2, 16)), -0.4, 0.0), -0.12, 0.12)
    vertical_vel = jnp.clip(jax.random.uniform(key_of[5], (LEV, NY, NX), jnp.float32, -0.12, 0.12) * shard_levels(key_of[5], (LEV, NY, NX), ((1, 2), (2, 16)), -0.4, 0.0), -0.12, 0.12)
    diffusivity = jnp.clip(0.01 + 0.03 * jax.random.uniform(key_of[6], (LEV, NY, NX), jnp.float32) ** shard_levels(key_of[6], (LEV, NY, NX), ((1, 2), (2, 16)), -0.2, 0.2), 0.01, 0.04)
    sea_mask = plant((jax.random.randint(key_of[7], (LEV, NY, NX), 0, 5) < 4).astype(jnp.int32), jax.random.fold_in(key_of[7], 1), 0, 1)
    reaction_rate = jnp.clip(jnp.exp(jax.random.uniform(key_of[8], (NTR, LEV), jnp.float32, math.log(0.05), math.log(0.5))), 0.05, 0.5)
    fold_partner = draw_fold_partner(jax.random.fold_in(key_of[10], 71), 0)
    return dict(tracer_start=tracer_start, source=source, target=target, east_vel=east_vel, north_vel=north_vel, vertical_vel=vertical_vel, diffusivity=diffusivity, sea_mask=sea_mask, reaction_rate=reaction_rate, fold_partner=fold_partner)


def upwind_pair(velocity, mixing, face_sea):
    flow_rate = velocity * face_sea
    mixing_part = mixing * face_sea
    return (jnp.maximum(flow_rate, 0.0) + mixing_part, jnp.minimum(flow_rate, 0.0) - mixing_part)

def next_row(values, axis):
    upper = lax.slice_in_dim(values, 1, values.shape[axis], axis=axis)
    empty = jnp.zeros_like(lax.slice_in_dim(values, 0, 1, axis=axis))
    return jnp.concatenate([upper, empty], axis)

def prev_row(values, axis):
    lower = lax.slice_in_dim(values, 0, values.shape[axis] - 1, axis=axis)
    empty = jnp.zeros_like(lax.slice_in_dim(values, 0, 1, axis=axis))
    return jnp.concatenate([empty, lower], axis)

def reference(tracer_start, source, target, east_vel, north_vel, vertical_vel, diffusivity, sea_mask, reaction_rate, fold_partner):
    ocean = sea_mask.astype(jnp.float32)
    east_own, east_next = upwind_pair(east_vel, 0.5 * (diffusivity + jnp.roll(diffusivity, -1, 2)), ocean * jnp.roll(ocean, -1, 2))
    north_own, north_next = upwind_pair(north_vel, 0.5 * (diffusivity + next_row(diffusivity, 1)), ocean * next_row(ocean, 1))
    up_own, up_next = upwind_pair(vertical_vel, 0.5 * (diffusivity + next_row(diffusivity, 0)), ocean * next_row(ocean, 0))
    top_vel = north_vel[:, -1, :]
    top_mix = diffusivity[:, -1, :]
    top_sea = ocean[:, -1, :]
    fold_own, fold_next = upwind_pair(0.5 * (top_vel - jnp.take(top_vel, fold_partner, axis=1)), 0.5 * (top_mix + jnp.take(top_mix, fold_partner, axis=1)), top_sea * jnp.take(top_sea, fold_partner, axis=1))

    def one_tracer(inputs):
        start, forcing, observed, rates = inputs
        decay_rate = rates[:, None, None]

        def divergence(quantity):
            east_flux = east_own * quantity + east_next * jnp.roll(quantity, -1, 2)
            north_flux = north_own * quantity + north_next * next_row(quantity, 1)
            top_row = quantity[:, -1, :]
            fold_flux = fold_own * top_row + fold_next * jnp.take(top_row, fold_partner, axis=1)
            north_flux = north_flux.at[:, -1, :].add(fold_flux)
            up_flux = up_own * quantity + up_next * next_row(quantity, 0)
            return east_flux - jnp.roll(east_flux, 1, 2) + (north_flux - prev_row(north_flux, 1)) + (up_flux - prev_row(up_flux, 0))

        def advance(quantity):
            uptake = decay_rate * quantity / jnp.sqrt(1.0 + quantity * quantity)
            return ocean * (quantity - divergence(quantity) - uptake + forcing)
        states = [start]
        for repeat in range(STEPS):
            states.append(advance(states[-1]))
        adjoint = ocean * (states[-1] - observed)
        gradient = ocean * adjoint
        for backward in range(STEPS - 1, 0, -1):
            unused, pull = jax.vjp(advance, states[backward])
            adjoint = pull(adjoint)[0]
            gradient = gradient + ocean * adjoint
        return gradient
    source_grad = lax.map(one_tracer, (tracer_start, source, target, reaction_rate))
    grad_norm = jnp.sqrt(jnp.sum(source_grad * source_grad))
    return (source_grad, grad_norm)
```

```python
import functools

import jax
import jax.numpy as jnp
from jax import lax
from jax.experimental import pallas as pl
from jax.experimental.pallas import tpu as pltpu
from jax.sharding import PartitionSpec as P

STEPS = 4
UNROLL = 4
NEAR = (-1, 1, 2, 3)
F32 = jnp.float32


def upwind_pair(velocity, mixing, face_sea):
    flow_rate = velocity * face_sea
    mixing_part = mixing * face_sea
    return (jnp.maximum(flow_rate, 0.0) + mixing_part, jnp.minimum(flow_rate, 0.0) - mixing_part)


def kernel(
    lon_n,
    lat_n,
    start_ref,
    source_ref,
    target_ref,
    east_ref,
    north_ref,
    vert_ref,
    diff_ref,
    mask_ref,
    rate_ref,
    fold_ref,
    grad_ref,
    norm_ref,
    states,
    ocean_ref,
    cen,
    eo,
    en,
    wo,
    wn,
    no,
    nn,
    so,
    sn,
    uo,
    un,
    send_west,
    send_east,
    send_top,
    send_low,
    picked,
    got_lon,
    got_lat,
    got_far,
    got_near,
    sum_a,
    sum_b,
    sum_c,
    send_sem,
    recv_sem,
    sum_send,
    sum_recv,
):
    ntr, lev, rows, cols = start_ref.shape
    groups = lon_n // 4
    lon = lax.axis_index("lon")
    lat = lax.axis_index("lat")

    def at(lon_to, lat_to):
        return {"lon": lon_to, "lat": lat_to}

    def wrap(index, count):
        return lax.rem(index + 2 * count, count)

    low4 = lax.rem(lon, 4)
    high4 = lon // 4
    far = [wrap(4 * k - lon, lon_n) for k in range(groups)]

    from_ids = [(wrap(lon - 1, lon_n), lat), (wrap(lon + 1, lon_n), lat)]
    from_ids += [(lon, wrap(lat - 1, lat_n)), (lon, wrap(lat + 1, lat_n))]
    from_ids += [(wrap(lon - j, lon_n), lat) for j in NEAR]
    from_ids += [(high4 * 4 + wrap(low4 - j, 4), lat) for j in range(1, 4)]
    from_ids += [(wrap(lon - 4 * k, lon_n), lat) for k in range(1, groups)]
    from_ids += [(lon, wrap(lat - j, lat_n)) for j in range(1, lat_n)]
    barrier = pltpu.get_barrier_semaphore()
    for lon_from, lat_from in from_ids:
        pl.semaphore_signal(
            barrier, inc=1, device_id=at(lon_from, lat_from), device_id_type=pl.DeviceIdType.MESH
        )
    for k in range(groups):

        @pl.when(far[k] != lon)
        def _():
            pl.semaphore_signal(
                barrier, inc=1, device_id=at(far[k], lat), device_id_type=pl.DeviceIdType.MESH
            )

    peers = len(from_ids)
    for k in range(groups):
        peers = peers + (far[k] != lon).astype(jnp.int32)
    pl.semaphore_wait(barrier, peers)

    lane = lax.broadcasted_iota(jnp.int32, (rows, cols), 1)
    row = lax.broadcasted_iota(jnp.int32, (rows, cols), 0)
    is_top = (lat == lat_n - 1).astype(F32)
    not_top = 1.0 - is_top
    not_low = (lat != 0).astype(F32)

    lane1 = lax.broadcasted_iota(jnp.int32, (1, cols), 1)
    nx = lon_n * cols
    offset = fold_ref[...] + lane1 + lon * cols
    offset = jnp.where(offset >= nx, offset - nx, offset)
    offset = jnp.where(offset >= nx, offset - nx, offset)
    far_mask = []
    rest = offset
    for k in range(groups):
        inside = (offset >= 4 * k * cols) & (offset < 4 * (k + 1) * cols)
        far_mask.append(inside)
        rest = jnp.where(inside, offset - 4 * k * cols, rest)
    near_mask = []
    within = rest
    for j in range(4):
        inside = (rest >= j * cols) & (rest < (j + 1) * cols)
        near_mask.append(inside)
        within = jnp.where(inside, rest - j * cols, within)
    column = lax.broadcasted_iota(jnp.int32, (2 * cols, cols), 0)
    pick = (column == (within - lane1 + cols)).astype(F32)

    def remote(src, dst, e, slot, where):
        return pltpu.make_async_remote_copy(
            src_ref=src,
            dst_ref=dst,
            send_sem=send_sem.at[e, slot],
            recv_sem=recv_sem.at[e, slot],
            device_id=where,
            device_id_type=pl.DeviceIdType.MESH,
        )

    def sides(e):
        return [
            remote(send_east.at[e], got_lon.at[e, 0], e, 0, at(wrap(lon + 1, lon_n), lat)),
            remote(send_west.at[e], got_lon.at[e, 1], e, 1, at(wrap(lon - 1, lon_n), lat)),
            remote(send_top.at[e], got_lat.at[e, 0], e, 2, at(lon, wrap(lat + 1, lat_n))),
            remote(send_low.at[e], got_lat.at[e, 1], e, 3, at(lon, wrap(lat - 1, lat_n))),
        ]

    def far_copy(e, k):
        return remote(send_top.at[e], got_far.at[e, k], e, 8 + k, at(far[k], lat))

    def near_copies(e):
        return [
            remote(picked.at[e], got_near.at[e, i], e, 4 + i, at(wrap(lon + j, lon_n), lat))
            for i, j in enumerate(NEAR)
        ]

    def start(e, get_col, get_row):
        for t in range(ntr):
            send_top[e, pl.ds(t * lev, lev), :] = get_row(t, rows - 1)
            send_low[e, pl.ds(t * lev, lev), :] = get_row(t, 0)
        for k in range(groups):

            @pl.when(far[k] != lon)
            def _():
                far_copy(e, k).start()

            @pl.when(far[k] == lon)
            def _():
                got_far[e, k] = send_top[e]

        copies = sides(e)
        copies[2].start()
        copies[3].start()

        def body(level, carry):
            west, east = carry
            for t in range(ntr):
                value = get_col(t, level)
                here = lane == level + t * lev
                west = jnp.where(here, value[:, 0:1], west)
                east = jnp.where(here, value[:, cols - 1 : cols], east)
            return west, east

        blank = jnp.zeros((rows, cols), F32)
        west, east = lax.fori_loop(0, lev, body, (blank, blank), unroll=UNROLL)
        send_west[e] = west
        send_east[e] = east
        copies[0].start()
        copies[1].start()

    def fold_far(e):
        for k in range(groups):

            @pl.when(far[k] != lon)
            def _():
                far_copy(e, k).wait()

        chosen = got_far[e, 0]
        for k in range(1, groups):
            chosen = jnp.where(far_mask[k], got_far[e, k], chosen)
        picked[e] = chosen
        for copy in near_copies(e):
            copy.start()

    def fold_near(e):
        for copy in near_copies(e):
            copy.wait()
        by_shift = {0: picked[e]}
        for i, j in enumerate(NEAR):
            by_shift[j] = got_near[e, i]
        upper = by_shift[0]
        lower = by_shift[-1]
        for j in range(1, 4):
            upper = jnp.where(near_mask[j], by_shift[j], upper)
            lower = jnp.where(near_mask[j], by_shift[j - 1], lower)
        both = jnp.concatenate([lower, upper], axis=1)
        return jnp.dot(
            both, pick, preferred_element_type=F32, precision=lax.Precision.HIGHEST
        )

    def wait_sides(e):
        for copy in sides(e):
            copy.wait()

    def shift_lon(value, from_west, from_east):
        west = jnp.where(lane == 0, from_west, pltpu.roll(value, 1, 1))
        east = jnp.where(lane == cols - 1, from_east, pltpu.roll(value, cols - 1, 1))
        return west, east

    def shift_lat(value, from_south, from_north):
        south = jnp.where(row == 0, from_south, pltpu.roll(value, 1, 0))
        north = jnp.where(row == rows - 1, from_north, pltpu.roll(value, rows - 1, 0))
        return south, north

    ocean_ref[...] = mask_ref[...].astype(F32)
    east_set = (east_ref, diff_ref, ocean_ref)
    north_set = (north_ref, diff_ref, ocean_ref)
    start(0, lambda t, l: east_set[t][l], lambda t, r: north_set[t][:, r, :])
    start(1, lambda t, l: start_ref[t, l], lambda t, r: start_ref[t, :, r, :])
    fold_far(0)
    fold_far(1)
    wait_sides(0)
    across = fold_near(0)
    got_far[0, 0] = across

    uo[0] = jnp.zeros((rows, cols), F32)
    un[0] = jnp.zeros((rows, cols), F32)

    def coefficients(level, carry):
        west, east = carry
        above = jnp.minimum(level + 1, lev - 1)
        ev, nv, vv = east_ref[level], north_ref[level], vert_ref[level]
        d, o = diff_ref[level], ocean_ref[level]

        def lon_side(t):
            return west[:, t * lev : t * lev + 1], east[:, t * lev : t * lev + 1]

        def lat_row(side, t):
            return got_lat[0, side, pl.ds(t * lev + level, 1), :]

        def fold_row(t):
            return got_far[0, 0, pl.ds(t * lev + level, 1), :]

        ev_w, unused = shift_lon(ev, *lon_side(0))
        d_w, d_e = shift_lon(d, *lon_side(1))
        o_w, o_e = shift_lon(o, *lon_side(2))
        e_own, e_next = upwind_pair(ev, 0.5 * (d + d_e), o * o_e)
        w_own, w_next = upwind_pair(ev_w, 0.5 * (d_w + d), o_w * o)
        nv_s, unused = shift_lat(nv, lat_row(0, 0), lat_row(0, 0))
        d_s, d_n = shift_lat(d, lat_row(0, 1), not_top * lat_row(1, 1) + is_top * fold_row(1))
        o_s, o_n = shift_lat(
            o, not_low * lat_row(0, 2), not_top * lat_row(1, 2) + is_top * fold_row(2)
        )
        across_vel = is_top * (0.5 * (nv - fold_row(0))) + not_top * nv
        nq = jnp.where(row == rows - 1, across_vel, nv)
        n_own, n_next = upwind_pair(nq, 0.5 * (d + d_n), o * o_n)
        s_own, s_next = upwind_pair(nv_s, 0.5 * (d_s + d), o_s * o)
        inner = (level < lev - 1).astype(F32)
        u_own, u_next = upwind_pair(
            vv, 0.5 * (d + diff_ref[above]), o * ocean_ref[above] * inner
        )
        eo[level], en[level] = e_own, e_next
        wo[level], wn[level] = w_own, w_next
        no[level], nn[level] = n_own, n_next
        so[level], sn[level] = s_own, s_next
        uo[level + 1], un[level + 1] = u_own, u_next
        cen[level] = o - ((e_own - w_next) + (n_own - s_next) + (u_own - un[level]))
        return pltpu.roll(west, cols - 1, 1), pltpu.roll(east, cols - 1, 1)

    lax.fori_loop(0, lev, coefficients, (got_lon[0, 0], got_lon[0, 1]), unroll=UNROLL)

    last = 2 * STEPS - 2
    for step in range(last + 1):
        e = step + 1
        forward = step < STEPS
        src = start_ref if step == 0 else states.at[step - 1]
        dst = grad_ref if step == last else states.at[step]
        if step:
            fold_far(e)
        wait_sides(e)

        def advance(level, carry):
            west, east = carry
            above = jnp.minimum(level + 1, lev - 1)
            below = jnp.maximum(level - 1, 0)
            o = ocean_ref[level]
            middle = cen[level]
            if forward:
                k_e, k_w, k_n, k_s = en[level], wo[level], nn[level], so[level]
                k_u, k_d = un[level + 1], uo[level]
            else:
                k_e, k_w, k_n, k_s = eo[level], wn[level], no[level], sn[level]
                k_u, k_d = uo[level + 1], un[level]
            for t in range(ntr):
                value = src[t, level]
                v_w, v_e = shift_lon(
                    value, west[:, t * lev : t * lev + 1], east[:, t * lev : t * lev + 1]
                )
                v_s, v_n = shift_lat(
                    value,
                    got_lat[e, 0, pl.ds(t * lev + level, 1), :],
                    not_top * got_lat[e, 1, pl.ds(t * lev + level, 1), :],
                )
                v_u, v_d = src[t, above], src[t, below]
                out_flow = (k_e * v_e - k_w * v_w) + (k_n * v_n - k_s * v_s) + (k_u * v_u - k_d * v_d)
                rate = rate_ref[t, level]
                if forward:
                    root = lax.rsqrt(1.0 + value * value)
                    new = middle * value - out_flow + o * (
                        source_ref[t, level] - rate * (value * root)
                    )
                    if step == STEPS - 1:
                        new = new - o * target_ref[t, level]
                else:
                    state = states[2 * STEPS - 2 - step, t, level]
                    root = lax.rsqrt(1.0 + state * state)
                    new = middle * value + out_flow - rate * (root * root * root) * value
                    if step == last:
                        for other in range(STEPS - 1, last):
                            new = new + states[other, t, level]
                dst[t, level] = new
            return pltpu.roll(west, cols - 1, 1), pltpu.roll(east, cols - 1, 1)

        lax.fori_loop(0, lev, advance, (got_lon[e, 0], got_lon[e, 1]), unroll=UNROLL)
        across = fold_near(e)
        if forward:
            top_gain = -is_top * nn[:, rows - 1, :]
        else:
            top_gain = is_top * no[:, rows - 1, :]
        for t in range(ntr):
            dst[t, :, rows - 1, :] = (
                dst[t, :, rows - 1, :] + top_gain * across[t * lev : (t + 1) * lev, :]
            )
        if step < last:
            start(e + 1, lambda t, l: dst[t, l], lambda t, r: dst[t, :, r, :])

    def square(level, total):
        for t in range(ntr):
            value = grad_ref[t, level]
            total = total + value * value
        return total

    total = lax.fori_loop(0, lev, square, jnp.zeros((rows, cols), F32), unroll=UNROLL)

    def share(total, slots, mine, sem, targets):
        slots[mine] = total
        copies = [
            pltpu.make_async_remote_copy(
                src_ref=slots.at[mine],
                dst_ref=slots.at[mine],
                send_sem=sum_send.at[sem + i],
                recv_sem=sum_recv.at[sem + i],
                device_id=where,
                device_id_type=pl.DeviceIdType.MESH,
            )
            for i, where in enumerate(targets)
        ]
        for copy in copies:
            copy.start()
        for copy in copies:
            copy.wait()
        total = slots[0]
        for i in range(1, slots.shape[0]):
            total = total + slots[i]
        return total

    small = total[0:8]
    for r in range(8, rows, 8):
        small = small + total[r : r + 8]
    small = share(
        small, sum_a, low4, 0, [at(high4 * 4 + wrap(low4 + j, 4), lat) for j in range(1, 4)]
    )
    small = share(
        small, sum_b, high4, 3, [at(wrap(lon + 4 * k, lon_n), lat) for k in range(1, groups)]
    )
    small = share(
        small, sum_c, lat, 2 + groups, [at(lon, wrap(lat + j, lat_n)) for j in range(1, lat_n)]
    )
    norm_ref[...] = jnp.sqrt(jnp.sum(jnp.sum(small, axis=0, keepdims=True), axis=1, keepdims=True))


def on_device(lon_n, lat_n, *args):
    ntr, lev, rows, cols = args[0].shape
    fold = args[9].reshape(1, cols)
    groups = lon_n // 4
    exchanges = 2 * STEPS
    slots = 8 + groups
    vmem = pl.BlockSpec(memory_space=pltpu.VMEM)
    plane = pltpu.VMEM((lev, rows, cols), F32)
    tall = pltpu.VMEM((lev + 1, rows, cols), F32)
    column = pltpu.VMEM((exchanges, rows, cols), F32)
    line = pltpu.VMEM((exchanges, ntr * lev, cols), F32)
    grad, norm = pl.pallas_call(
        functools.partial(kernel, lon_n, lat_n),
        out_shape=(
            jax.ShapeDtypeStruct(args[0].shape, F32),
            jax.ShapeDtypeStruct((1, 1), F32),
        ),
        in_specs=[vmem] * 8 + [pl.BlockSpec(memory_space=pltpu.SMEM), vmem],
        out_specs=(vmem, vmem),
        scratch_shapes=[
            pltpu.VMEM((2 * STEPS - 2, ntr, lev, rows, cols), F32),
            plane,
            *[plane] * 9,
            tall,
            tall,
            column,
            column,
            line,
            line,
            line,
            pltpu.VMEM((exchanges, 2, rows, cols), F32),
            pltpu.VMEM((exchanges, 2, ntr * lev, cols), F32),
            pltpu.VMEM((exchanges, groups, ntr * lev, cols), F32),
            pltpu.VMEM((exchanges, len(NEAR), ntr * lev, cols), F32),
            pltpu.VMEM((4, 8, cols), F32),
            pltpu.VMEM((groups, 8, cols), F32),
            pltpu.VMEM((lat_n, 8, cols), F32),
            pltpu.SemaphoreType.DMA((exchanges, slots)),
            pltpu.SemaphoreType.DMA((exchanges, slots)),
            pltpu.SemaphoreType.DMA((2 + groups + lat_n,)),
            pltpu.SemaphoreType.DMA((2 + groups + lat_n,)),
        ],
        compiler_params=pltpu.CompilerParams(
            collective_id=0, has_side_effects=True, vmem_limit_bytes=40 * 1024 * 1024
        ),
    )(*args[:9], fold)
    return grad, norm[0, 0]


def solution(mesh):
    field = P(None, None, "lat", "lon")
    static = P(None, "lat", "lon")
    return jax.shard_map(
        functools.partial(on_device, mesh.shape["lon"], mesh.shape["lat"]),
        mesh=mesh,
        in_specs=(field, field, field, *[static] * 5, P(), P("lon")),
        out_specs=(field, P()),
        check_vma=False,
    )
```

```python
import functools

import jax
import jax.numpy as jnp
from jax import lax
from jax.experimental import pallas as pl
from jax.experimental.pallas import tpu as pltpu
from jax.sharding import PartitionSpec as P

STEPS = 4
UNROLL = 4
NEAR = (-1, 1, 2, 3)
F32 = jnp.float32


def upwind_pair(velocity, mixing, face_sea):
    flow_rate = velocity * face_sea
    mixing_part = mixing * face_sea
    return (jnp.maximum(flow_rate, 0.0) + mixing_part, jnp.minimum(flow_rate, 0.0) - mixing_part)


def kernel(
    lon_n,
    lat_n,
    start_hbm,
    source_hbm,
    target_hbm,
    east_hbm,
    north_hbm,
    vert_hbm,
    diff_hbm,
    mask_hbm,
    rate_hbm,
    fold_hbm,
    grad_ref,
    norm_ref,
    start_ref,
    source_ref,
    target_ref,
    east_ref,
    north_ref,
    vert_ref,
    diff_ref,
    mask_ref,
    rate_ref,
    fold_ref,
    load_sem,
    states,
    ocean_ref,
    cen,
    eo,
    en,
    wo,
    wn,
    no,
    nn,
    so,
    sn,
    uo,
    un,
    send_west,
    send_east,
    send_top,
    send_low,
    picked,
    got_lon,
    got_lat,
    got_far,
    got_near,
    sum_a,
    sum_b,
    send_sem,
    recv_sem,
    sum_send,
    sum_recv,
):
    ntr, lev, rows, cols = start_ref.shape
    groups = lon_n // 4
    pairs = {
        "mask": (mask_hbm, mask_ref),
        "diff": (diff_hbm, diff_ref),
        "north": (north_hbm, north_ref),
        "east": (east_hbm, east_ref),
        "start": (start_hbm, start_ref),
        "fold": (fold_hbm, fold_ref),
        "vert": (vert_hbm, vert_ref),
        "rate": (rate_hbm, rate_ref),
        "source": (source_hbm, source_ref),
        "target": (target_hbm, target_ref),
    }
    loads = {
        name: pltpu.make_async_copy(src, dst, load_sem.at[i])
        for i, (name, (src, dst)) in enumerate(pairs.items())
    }
    for copy in loads.values():
        copy.start()
    lon = lax.axis_index("lon")
    lat = lax.axis_index("lat")

    def at(lon_to, lat_to):
        return {"lon": lon_to, "lat": lat_to}

    def wrap(index, count):
        return lax.rem(index + 2 * count, count)

    low4 = lax.rem(lon, 4)
    high4 = lon // 4
    far = [wrap(4 * k - lon, lon_n) for k in range(groups)]

    from_ids = [(wrap(lon - 1, lon_n), lat), (wrap(lon + 1, lon_n), lat)]
    from_ids += [(lon, wrap(lat - 1, lat_n)), (lon, wrap(lat + 1, lat_n))]
    from_ids += [(wrap(lon - j, lon_n), lat) for j in NEAR]
    from_ids += [
        (high4 * 4 + wrap(low4 - j, 4), wrap(lat - i, lat_n))
        for i in range(lat_n)
        for j in range(4)
        if i or j
    ]
    from_ids += [(wrap(lon - 4 * k, lon_n), lat) for k in range(1, groups)]
    barrier = pltpu.get_barrier_semaphore()
    for lon_from, lat_from in from_ids:
        pl.semaphore_signal(
            barrier, inc=1, device_id=at(lon_from, lat_from), device_id_type=pl.DeviceIdType.MESH
        )
    for k in range(groups):

        @pl.when(far[k] != lon)
        def _():
            pl.semaphore_signal(
                barrier, inc=1, device_id=at(far[k], lat), device_id_type=pl.DeviceIdType.MESH
            )

    peers = len(from_ids)
    for k in range(groups):
        peers = peers + (far[k] != lon).astype(jnp.int32)
    pl.semaphore_wait(barrier, peers)

    lane = lax.broadcasted_iota(jnp.int32, (rows, cols), 1)
    row = lax.broadcasted_iota(jnp.int32, (rows, cols), 0)
    is_top = (lat == lat_n - 1).astype(F32)
    not_top = 1.0 - is_top
    not_low = (lat != 0).astype(F32)

    def remote(src, dst, e, slot, where):
        return pltpu.make_async_remote_copy(
            src_ref=src,
            dst_ref=dst,
            send_sem=send_sem.at[e, slot],
            recv_sem=recv_sem.at[e, slot],
            device_id=where,
            device_id_type=pl.DeviceIdType.MESH,
        )

    def sides(e):
        return [
            remote(send_east.at[e], got_lon.at[e, 0], e, 0, at(wrap(lon + 1, lon_n), lat)),
            remote(send_west.at[e], got_lon.at[e, 1], e, 1, at(wrap(lon - 1, lon_n), lat)),
            remote(send_top.at[e], got_lat.at[e, 0], e, 2, at(lon, wrap(lat + 1, lat_n))),
            remote(send_low.at[e], got_lat.at[e, 1], e, 3, at(lon, wrap(lat - 1, lat_n))),
        ]

    def far_copy(e, k):
        return remote(send_top.at[e], got_far.at[e, k], e, 8 + k, at(far[k], lat))

    def near_copies(e):
        return [
            remote(picked.at[e], got_near.at[e, i], e, 4 + i, at(wrap(lon + j, lon_n), lat))
            for i, j in enumerate(NEAR)
        ]

    def send_tops(e):
        for k in range(groups):

            @pl.when(far[k] != lon)
            def _():
                far_copy(e, k).start()

            @pl.when(far[k] == lon)
            def _():
                got_far[e, k] = send_top[e]

        sides(e)[2].start()

    def send_lows(e):
        sides(e)[3].start()

    def send_columns(e, get_col):
        def body(level, carry):
            west, east = carry
            for t in range(ntr):
                value = get_col(t, level)
                here = lane == level + t * lev
                west = jnp.where(here, value[:, 0:1], west)
                east = jnp.where(here, value[:, cols - 1 : cols], east)
            return west, east

        blank = jnp.zeros((rows, cols), F32)
        west, east = lax.fori_loop(0, lev, body, (blank, blank), unroll=UNROLL)
        send_west[e] = west
        send_east[e] = east
        sides(e)[0].start()
        sides(e)[1].start()

    def start(e, get_col, get_row):
        for t in range(ntr):
            send_top[e, pl.ds(t * lev, lev), :] = get_row(t, rows - 1)
        send_tops(e)
        for t in range(ntr):
            send_low[e, pl.ds(t * lev, lev), :] = get_row(t, 0)
        send_lows(e)
        send_columns(e, get_col)

    def fold_far(e):
        for k in range(groups):

            @pl.when(far[k] != lon)
            def _():
                far_copy(e, k).wait()

        chosen = got_far[e, 0]
        for k in range(1, groups):
            chosen = jnp.where(far_mask[k], got_far[e, k], chosen)
        picked[e] = chosen
        for copy in near_copies(e):
            copy.start()

    def fold_near(e):
        for copy in near_copies(e):
            copy.wait()
        by_shift = {0: picked[e]}
        for i, j in enumerate(NEAR):
            by_shift[j] = got_near[e, i]
        upper = by_shift[0]
        lower = by_shift[-1]
        for j in range(1, 4):
            upper = jnp.where(near_mask[j], by_shift[j], upper)
            lower = jnp.where(near_mask[j], by_shift[j - 1], lower)
        both = jnp.concatenate([lower, upper], axis=1)
        high = both.astype(jnp.bfloat16)
        rest1 = both - high.astype(F32)
        mid = rest1.astype(jnp.bfloat16)
        low = (rest1 - mid.astype(F32)).astype(jnp.bfloat16)
        parts = jnp.concatenate([high, mid, low], axis=0)
        found = jnp.dot(parts, pick, preferred_element_type=F32)
        count = ntr * lev
        return found[0:count] + found[count : 2 * count] + found[2 * count :]

    def wait_sides(e):
        for copy in sides(e):
            copy.wait()

    def shift_lon(value, from_west, from_east):
        west = jnp.where(lane == 0, from_west, pltpu.roll(value, 1, 1))
        east = jnp.where(lane == cols - 1, from_east, pltpu.roll(value, cols - 1, 1))
        return west, east

    def shift_lat(value, from_south, from_north):
        south = jnp.where(row == 0, from_south, pltpu.roll(value, 1, 0))
        north = jnp.where(row == rows - 1, from_north, pltpu.roll(value, rows - 1, 0))
        return south, north

    for name in ("mask", "diff", "north", "east"):
        loads[name].wait()
    ocean_ref[...] = mask_ref[...].astype(F32)
    east_set = (east_ref, diff_ref, ocean_ref)
    north_set = (north_ref, diff_ref, ocean_ref)
    start(0, lambda t, l: east_set[t][l], lambda t, r: north_set[t][:, r, :])
    loads["start"].wait()
    start(1, lambda t, l: start_ref[t, l], lambda t, r: start_ref[t, :, r, :])
    loads["fold"].wait()
    lane1 = lax.broadcasted_iota(jnp.int32, (1, cols), 1)
    nx = lon_n * cols
    offset = fold_ref[...] + lane1 + lon * cols
    offset = jnp.where(offset >= nx, offset - nx, offset)
    offset = jnp.where(offset >= nx, offset - nx, offset)
    far_mask = []
    rest = offset
    for k in range(groups):
        inside = (offset >= 4 * k * cols) & (offset < 4 * (k + 1) * cols)
        far_mask.append(inside)
        rest = jnp.where(inside, offset - 4 * k * cols, rest)
    near_mask = []
    within = rest
    for j in range(4):
        inside = (rest >= j * cols) & (rest < (j + 1) * cols)
        near_mask.append(inside)
        within = jnp.where(inside, rest - j * cols, within)
    column = lax.broadcasted_iota(jnp.int32, (2 * cols, cols), 0)
    pick = (column == (within - lane1 + cols)).astype(F32).astype(jnp.bfloat16)

    for name in ("vert", "rate", "source", "target"):
        loads[name].wait()
    fold_far(0)
    fold_far(1)
    wait_sides(0)
    across = fold_near(0)
    got_far[0, 0] = across

    uo[0] = jnp.zeros((rows, cols), F32)
    un[0] = jnp.zeros((rows, cols), F32)

    def coefficients(level, carry):
        west, east = carry
        above = jnp.minimum(level + 1, lev - 1)
        ev, nv, vv = east_ref[level], north_ref[level], vert_ref[level]
        d, o = diff_ref[level], ocean_ref[level]

        def lon_side(t):
            return west[:, t * lev : t * lev + 1], east[:, t * lev : t * lev + 1]

        def lat_row(side, t):
            return got_lat[0, side, pl.ds(t * lev + level, 1), :]

        def fold_row(t):
            return got_far[0, 0, pl.ds(t * lev + level, 1), :]

        ev_w, unused = shift_lon(ev, *lon_side(0))
        d_w, d_e = shift_lon(d, *lon_side(1))
        o_w, o_e = shift_lon(o, *lon_side(2))
        e_own, e_next = upwind_pair(ev, 0.5 * (d + d_e), o * o_e)
        w_own, w_next = upwind_pair(ev_w, 0.5 * (d_w + d), o_w * o)
        nv_s, unused = shift_lat(nv, lat_row(0, 0), lat_row(0, 0))
        d_s, d_n = shift_lat(d, lat_row(0, 1), not_top * lat_row(1, 1) + is_top * fold_row(1))
        o_s, o_n = shift_lat(
            o, not_low * lat_row(0, 2), not_top * lat_row(1, 2) + is_top * fold_row(2)
        )
        across_vel = is_top * (0.5 * (nv - fold_row(0))) + not_top * nv
        nq = jnp.where(row == rows - 1, across_vel, nv)
        n_own, n_next = upwind_pair(nq, 0.5 * (d + d_n), o * o_n)
        s_own, s_next = upwind_pair(nv_s, 0.5 * (d_s + d), o_s * o)
        inner = (level < lev - 1).astype(F32)
        u_own, u_next = upwind_pair(
            vv, 0.5 * (d + diff_ref[above]), o * ocean_ref[above] * inner
        )
        eo[level], en[level] = e_own, e_next
        wo[level], wn[level] = w_own, w_next
        no[level], nn[level] = n_own, n_next
        so[level], sn[level] = s_own, s_next
        uo[level + 1], un[level + 1] = u_own, u_next
        cen[level] = o - ((e_own - w_next) + (n_own - s_next) + (u_own - un[level]))
        return pltpu.roll(west, cols - 1, 1), pltpu.roll(east, cols - 1, 1)

    lax.fori_loop(0, lev, coefficients, (got_lon[0, 0], got_lon[0, 1]), unroll=UNROLL)

    last = 2 * STEPS - 2
    for step in range(last + 1):
        e = step + 1
        forward = step < STEPS
        src = start_ref if step == 0 else states.at[step - 1]
        dst = grad_ref if step == last else states.at[step]
        if step:
            fold_far(e)
        wait_sides(e)

        def advance(level, carry):
            west, east = carry
            above = jnp.minimum(level + 1, lev - 1)
            below = jnp.maximum(level - 1, 0)
            o = ocean_ref[level]
            middle = cen[level]
            if forward:
                k_e, k_w, k_n, k_s = en[level], wo[level], nn[level], so[level]
                k_u, k_d = un[level + 1], uo[level]
            else:
                k_e, k_w, k_n, k_s = eo[level], wn[level], no[level], sn[level]
                k_u, k_d = uo[level + 1], un[level]
            for t in range(ntr):
                value = src[t, level]
                v_w, v_e = shift_lon(
                    value, west[:, t * lev : t * lev + 1], east[:, t * lev : t * lev + 1]
                )
                v_s, v_n = shift_lat(
                    value,
                    got_lat[e, 0, pl.ds(t * lev + level, 1), :],
                    not_top * got_lat[e, 1, pl.ds(t * lev + level, 1), :],
                )
                v_u, v_d = src[t, above], src[t, below]
                out_flow = (k_e * v_e - k_w * v_w) + (k_n * v_n - k_s * v_s) + (k_u * v_u - k_d * v_d)
                rate = rate_ref[t, level]
                if forward:
                    root = lax.rsqrt(1.0 + value * value)
                    new = middle * value - out_flow + o * (
                        source_ref[t, level] - rate * (value * root)
                    )
                    if step == STEPS - 1:
                        new = new - o * target_ref[t, level]
                else:
                    state = states[2 * STEPS - 2 - step, t, level]
                    root = lax.rsqrt(1.0 + state * state)
                    new = middle * value + out_flow - rate * (root * root * root) * value
                    if step == last:
                        for other in range(STEPS - 1, last):
                            new = new + states[other, t, level]
                dst[t, level] = new
            return pltpu.roll(west, cols - 1, 1), pltpu.roll(east, cols - 1, 1)

        lax.fori_loop(0, lev, advance, (got_lon[e, 0], got_lon[e, 1]), unroll=UNROLL)
        if step < last:
            for t in range(ntr):
                send_low[e + 1, pl.ds(t * lev, lev), :] = dst[t, :, 0, :]
            send_lows(e + 1)
        across = fold_near(e)
        if forward:
            top_gain = -is_top * nn[:, rows - 1, :]
        else:
            top_gain = is_top * no[:, rows - 1, :]
        tops = [
            dst[t, :, rows - 1, :] + top_gain * across[t * lev : (t + 1) * lev, :]
            for t in range(ntr)
        ]
        if step < last:
            for t in range(ntr):
                send_top[e + 1, pl.ds(t * lev, lev), :] = tops[t]
            send_tops(e + 1)
        for t in range(ntr):
            dst[t, :, rows - 1, :] = tops[t]
        if step < last:
            send_columns(e + 1, lambda t, l: dst[t, l])

    def square(level, total):
        for t in range(ntr):
            value = grad_ref[t, level]
            total = total + value * value
        return total

    total = lax.fori_loop(0, lev, square, jnp.zeros((rows, cols), F32), unroll=UNROLL)

    def share(total, slots, mine, sem, targets):
        slots[mine] = total
        copies = [
            pltpu.make_async_remote_copy(
                src_ref=slots.at[mine],
                dst_ref=slots.at[mine],
                send_sem=sum_send.at[sem + i],
                recv_sem=sum_recv.at[sem + i],
                device_id=where,
                device_id_type=pl.DeviceIdType.MESH,
            )
            for i, where in enumerate(targets)
        ]
        for copy in copies:
            copy.start()
        for copy in copies:
            copy.wait()
        total = slots[0]
        for i in range(1, slots.shape[0]):
            total = total + slots[i]
        return total

    small = total[0:8]
    for r in range(8, rows, 8):
        small = small + total[r : r + 8]
    near_ids = [
        at(high4 * 4 + wrap(low4 + j, 4), wrap(lat + i, lat_n))
        for i in range(lat_n)
        for j in range(4)
        if i or j
    ]
    far_ids = [at(wrap(lon + 4 * k, lon_n), lat) for k in range(1, groups)]
    small = share(small, sum_a, lat * 4 + low4, 0, near_ids)
    small = share(small, sum_b, high4, len(near_ids), far_ids)
    norm_ref[...] = jnp.sqrt(jnp.sum(jnp.sum(small, axis=0, keepdims=True), axis=1, keepdims=True))


def on_device(lon_n, lat_n, *args):
    ntr, lev, rows, cols = args[0].shape
    fold = args[9].reshape(1, cols)
    groups = lon_n // 4
    exchanges = 2 * STEPS
    slots = 8 + groups
    vmem = pl.BlockSpec(memory_space=pltpu.VMEM)
    plane = pltpu.VMEM((lev, rows, cols), F32)
    tall = pltpu.VMEM((lev + 1, rows, cols), F32)
    column = pltpu.VMEM((exchanges, rows, cols), F32)
    line = pltpu.VMEM((exchanges, ntr * lev, cols), F32)
    grad, norm = pl.pallas_call(
        functools.partial(kernel, lon_n, lat_n),
        out_shape=(
            jax.ShapeDtypeStruct(args[0].shape, F32),
            jax.ShapeDtypeStruct((1, 1), F32),
        ),
        in_specs=[pl.BlockSpec(memory_space=pltpu.HBM)] * 10,
        out_specs=(vmem, vmem),
        scratch_shapes=[
            *[pltpu.VMEM(a.shape, a.dtype) for a in args[:8]],
            pltpu.SMEM(args[8].shape, F32),
            pltpu.VMEM(fold.shape, jnp.int32),
            pltpu.SemaphoreType.DMA((10,)),
            pltpu.VMEM((2 * STEPS - 2, ntr, lev, rows, cols), F32),
            plane,
            *[plane] * 9,
            tall,
            tall,
            column,
            column,
            line,
            line,
            line,
            pltpu.VMEM((exchanges, 2, rows, cols), F32),
            pltpu.VMEM((exchanges, 2, ntr * lev, cols), F32),
            pltpu.VMEM((exchanges, groups, ntr * lev, cols), F32),
            pltpu.VMEM((exchanges, len(NEAR), ntr * lev, cols), F32),
            pltpu.VMEM((4 * lat_n, 8, cols), F32),
            pltpu.VMEM((groups, 8, cols), F32),
            pltpu.SemaphoreType.DMA((exchanges, slots)),
            pltpu.SemaphoreType.DMA((exchanges, slots)),
            pltpu.SemaphoreType.DMA((4 * lat_n + groups,)),
            pltpu.SemaphoreType.DMA((4 * lat_n + groups,)),
        ],
        compiler_params=pltpu.CompilerParams(
            collective_id=0, has_side_effects=True, vmem_limit_bytes=64 * 1024 * 1024 - 65536
        ),
    )(*args[:9], fold)
    return grad, norm[0, 0]


def solution(mesh):
    field = P(None, None, "lat", "lon")
    static = P(None, "lat", "lon")
    return jax.shard_map(
        functools.partial(on_device, mesh.shape["lon"], mesh.shape["lat"]),
        mesh=mesh,
        in_specs=(field, field, field, *[static] * 5, P(), P("lon")),
        out_specs=(field, P()),
        check_vma=False,
    )
```
